128 devices in a mesh: dp: 8 (over z, core), expert: 16 (over y, x).
Axes of the slice: x: 4, y: 4, z: 4, core: 2. Of those that a mesh axis runs over, the one named last changes fastest.
Arguments:
- tokens: bfloat16 [32768, 1024], P(('dp', 'expert')), may hold values from -6 to 6
- cotangent: bfloat16 [32768, 1024], P(('dp', 'expert')), may hold values from -6 to 6
- combine: float32 [32768, 2], P(('dp', 'expert')), may hold values from 0.2 to 1
- expert_ids: int32 [32768, 2], P(('dp', 'expert')), may hold values from 0 to 31, all different within a row; in each aligned block of 256 rows (0 to 255, 256 to 511, ...) at most 32 rows name the same one
- capacity: int32 [32], replicated, may hold values from 16 to 32, as said below
- weight_in: bfloat16 [1024, 32, 2048], P(None, 'expert'), may hold values from -0.1875 to 0.1875
- weight_down: bfloat16 [1024, 32, 1024], P(None, 'expert'), may hold values from -0.1875 to 0.1875
Outputs:
- token_grad: bfloat16 [32768, 1024], P(('dp', 'expert'))
- combine_grad: bfloat16 [32768, 2], P(('dp', 'expert'))
- inner_grad: float32 [1024, 32, 2048], P('dp', 'expert')
- down_grad: float32 [1024, 32, 1024], P('dp', 'expert')
The draws below stay inside these ranges and needn't reach their ends.
Inputs may be any that keep to these rules, and one draw needn't show every extreme that they name: Some expert has capacity 32. `expert_ids`: in the 256 rows of one device no expert is named more than 32 times.
All inputs are finite; a program needn't handle non-finite values.
Results may differ from the reference program's by a relative error of at most 0.015.
Values may be sent and summed in bfloat16 or wider, within the bound.
A program may use at most 128 MiB of HBM per device.

```python
import math
import jax
import jax.numpy as jnp
import numpy as np
from jax import lax

D = 1024
FF = 1024
TOK_DEV = 256
CAP = 32
EXPERTS = 32
TOKENS = 32768
N_DP = 8
N_EXPERT = 16


def draw_capacity(key, part):
    key = jax.random.fold_in(key, 11)
    first, second = jax.random.split(key)
    values = jax.random.randint(first, (EXPERTS,), CAP // 2, CAP + 1)
    chosen = jax.random.randint(second, (), 0, EXPERTS)
    return jnp.where(jnp.arange(EXPERTS) == chosen, CAP, values).astype(jnp.int32)


def steps_of(rng, dims, cuts, least, high):
    def one(dim, blocks):
        heights = jax.random.uniform(jax.random.fold_in(jax.random.fold_in(rng, 6), dim), (blocks,), jnp.float32, least / len(cuts), high / len(cuts))
        return jnp.repeat(jnp.exp(heights), dims[dim] // blocks).reshape((-1,) + (1,) * (len(dims) - dim - 1))

    level = one(*cuts[0])
    for cut in cuts[1:]:
        level = level * one(*cut)
    return level


def assign_block(key, own, number, rows, count, top, most, lean):
    sequence = jax.random.permutation(key, count)
    packed, ordinary = shares(count, rows * top, most, lean, True), shares(count, rows * top, most, lean, False)
    places = jnp.arange(count)

    def named(tallies, offset_by):
        used = int((tallies > 0).sum())
        fixed = max(1, used // 4)
        shifted = fixed + (places - fixed + offset_by * (used - fixed)) % max(1, count - fixed)
        return jnp.zeros((count,), jnp.int32).at[sequence[jnp.where(places < fixed, places, shifted)]].set(jnp.asarray(tallies, jnp.int32))

    tallies = jnp.where(number % 4 == 0, named(packed, number // 4), named(ordinary, number - number // 4 - 1))
    mixed = jax.random.permutation(jax.random.fold_in(own, 3), count)
    source_of, sink = mixed[0:count // 2 * 2:2], mixed[1:count // 2 * 2:2]
    margin = jnp.minimum(tallies[source_of] - 1, most - tallies[sink]) // 2
    margin = jnp.where((source_of == sequence[0]) | (sink == sequence[0]) | (tallies[sink] == 0), 0, jnp.maximum(margin, 0))
    shifted = jax.random.randint(jax.random.fold_in(own, 4), (count // 2,), 0, 1 << 20) % (margin + 1)
    tallies = tallies.at[source_of].add(-shifted).at[sink].add(shifted)
    members = jnp.searchsorted(jnp.cumsum(tallies), jnp.arange(rows * top), side="right").astype(jnp.int32)
    grid = members.reshape(top, rows).T
    grid = grid[jax.random.permutation(jax.random.fold_in(own, 1), rows)]
    offset_by = jax.random.randint(jax.random.fold_in(own, 2), (rows, 1), 0, top)
    return jnp.take_along_axis(grid, (jnp.arange(top)[None, :] + offset_by) % top, axis=1)


def shares(amount, total, reach, skew, full):
    weights = [(1 << 20) // math.isqrt(grade ** skew) + 1 for grade in range(1, amount + 1)]
    largest = reach if full else min(reach, max(-(-total // amount), total * weights[0] // sum(weights)))
    least = 1 if total - largest >= amount - 1 else 0
    holding, surplus = [largest] + [least] * (amount - 1), total - largest - least * (amount - 1)
    while surplus > 0:
        free = [i for i in range(1, amount) if holding[i] < largest] or [i for i in range(1, amount) if holding[i] < reach]
        whole, remaining = sum([weights[i] for i in free]), surplus
        for i in free:
            addition = min(reach - holding[i], max(1, remaining * weights[i] // whole), surplus)
            holding[i] = holding[i] + addition
            surplus = surplus - addition
    return np.array(holding)


def gaussian(stream_key, shape, width, most, cuts=(), kind=jnp.bfloat16):
    values = width * jax.random.normal(stream_key, shape, jnp.float32)
    if cuts:
        values = values * steps_of(stream_key, shape, cuts, -0.22, 0.18)
    return jnp.clip(values, -most, most).astype(kind)


def setup_inputs(seed: int = 0) -> dict:
    keys = jax.random.split(jax.random.key(seed), 8)
    tokens = gaussian(keys[0], (TOKENS, D), 1.0, 6.0, ((0, 128),))
    cotangent = gaussian(keys[1], (TOKENS, D), 1.0, 6.0, ((0, 128),))
    combine = jnp.clip(0.2 + 0.8 * jax.random.uniform(keys[2], (TOKENS, 2), jnp.float32) ** steps_of(keys[2], (TOKENS, 2), ((0, 128),), -0.2, 0.2), 0.2, 1.0)
    expert_ids_keys = jax.random.split(jax.random.fold_in(keys[3], 1), TOKENS // TOK_DEV)
    expert_ids_turns = jax.random.permutation(jax.random.fold_in(keys[3], 3), TOKENS // TOK_DEV)
    expert_ids = jax.vmap(lambda own, number: assign_block(jax.random.fold_in(keys[3], 2), own, number, TOK_DEV, EXPERTS, 2, CAP, 2))(expert_ids_keys, expert_ids_turns).reshape((TOKENS, 2))
    capacity = draw_capacity(jax.random.fold_in(keys[7], 71), 0)
    weight_in = gaussian(keys[5], (D, EXPERTS, 2 * FF), D ** -0.5, 0.1875, ((1, 16),))
    weight_down = gaussian(keys[6], (FF, EXPERTS, D), FF ** -0.5, 0.1875, ((1, 16),))
    return {"tokens": tokens, "cotangent": cotangent, "combine": combine, "expert_ids": expert_ids, "capacity": capacity, "weight_in": weight_in, "weight_down": weight_down}


def slot_layout(ids_block, capacity):
    flat = ids_block.reshape(-1).astype(jnp.int32)
    onehot = (flat[:, None] == jnp.arange(EXPERTS, dtype=jnp.int32)[None, :]).astype(jnp.int32)
    before = jnp.cumsum(onehot, axis=0) - onehot
    position = jnp.sum(before * onehot, axis=1)
    limit = jnp.sum(onehot * capacity[None, :], axis=1)
    live = position < limit
    target = jnp.where(live, flat * CAP + position, EXPERTS * CAP).astype(jnp.int32)
    count = flat.shape[0]
    source = jnp.full((EXPERTS * CAP + 1,), count, jnp.int32)
    source = source.at[target].set(jnp.arange(count, dtype=jnp.int32))[: EXPERTS * CAP]
    return target, source


def group_pass(weight_in, weight_down, capacity, group):
    tokens, cotangent, combine, ids = group
    targets, sources = jax.vmap(lambda b: slot_layout(b, capacity))(ids)
    zero_row = jnp.zeros((N_EXPERT, 1, D), jnp.bfloat16)
    padded_x = jnp.concatenate([tokens, zero_row], axis=1)
    padded_dy = jnp.concatenate([cotangent, zero_row], axis=1)
    token_of = sources // 2
    comb_flat = jnp.concatenate([combine.reshape(N_EXPERT, -1), jnp.zeros((N_EXPERT, 1), jnp.float32)], axis=1)
    slot_x = jnp.take_along_axis(padded_x, token_of[..., None], axis=1).reshape(N_EXPERT, EXPERTS, CAP, D)
    slot_dy = jnp.take_along_axis(padded_dy, token_of[..., None], axis=1).reshape(N_EXPERT, EXPERTS, CAP, D)
    slot_c = jnp.take_along_axis(comb_flat, sources, axis=1).astype(jnp.bfloat16).reshape(N_EXPERT, EXPERTS, CAP)
    win = weight_in.astype(jnp.float32)
    wdown = weight_down.astype(jnp.float32)
    pre = jnp.einsum('secd,def->secf', slot_x.astype(jnp.float32), win)
    gate = pre[..., :FF]
    upper = pre[..., FF:]
    sig = jax.nn.sigmoid(gate)
    act = gate * sig
    hidden = (act * upper).astype(jnp.bfloat16)
    output = jnp.einsum('secf,fed->secd', hidden.astype(jnp.float32), wdown)
    comb_slot = jnp.sum(slot_dy.astype(jnp.float32) * output, axis=-1).astype(jnp.bfloat16)
    scaled = (slot_c.astype(jnp.float32)[..., None] * slot_dy.astype(jnp.float32)).astype(jnp.bfloat16)
    dhidden = jnp.einsum('secd,fed->secf', scaled.astype(jnp.float32), wdown)
    dgate = dhidden * upper * sig * (1.0 + gate * (1.0 - sig))
    dpre = jnp.concatenate([dgate, dhidden * act], axis=-1).astype(jnp.bfloat16)
    slot_grad = jnp.einsum('secf,def->secd', dpre.astype(jnp.float32), win).astype(jnp.bfloat16)
    inner_part = jnp.einsum('secd,secf->def', slot_x.astype(jnp.float32), dpre.astype(jnp.float32)).astype(jnp.bfloat16)
    down_part = jnp.einsum('secf,secd->fed', hidden.astype(jnp.float32), scaled.astype(jnp.float32)).astype(jnp.bfloat16)
    back_x = jnp.concatenate([slot_grad.reshape(N_EXPERT, EXPERTS * CAP, D), zero_row], axis=1)
    back_c = jnp.concatenate([comb_slot.reshape(N_EXPERT, EXPERTS * CAP), jnp.zeros((N_EXPERT, 1), jnp.bfloat16)], axis=1)
    per_assign = jnp.take_along_axis(back_x, targets[..., None], axis=1).astype(jnp.float32)
    token_grad = per_assign.reshape(N_EXPERT, TOK_DEV, 2, D).sum(axis=2).astype(jnp.bfloat16)
    combine_grad = jnp.take_along_axis(back_c, targets, axis=1).reshape(N_EXPERT, TOK_DEV, 2)
    return token_grad, combine_grad, inner_part, down_part


def reference(tokens, cotangent, combine, expert_ids, capacity, weight_in, weight_down):
    grouped = (tokens.reshape(N_DP, N_EXPERT, TOK_DEV, D),
               cotangent.reshape(N_DP, N_EXPERT, TOK_DEV, D),
               combine.reshape(N_DP, N_EXPERT, TOK_DEV, 2),
               expert_ids.reshape(N_DP, N_EXPERT, TOK_DEV, 2))

    def step_fn(carry, group):
        token_grad, combine_grad, inner_part, down_part = group_pass(weight_in, weight_down, capacity, group)
        carry = (carry[0] + inner_part.astype(jnp.float32), carry[1] + down_part.astype(jnp.float32))
        return carry, (token_grad, combine_grad)

    start = (jnp.zeros((D, EXPERTS, 2 * FF), jnp.float32), jnp.zeros((FF, EXPERTS, D), jnp.float32))
    sums, outs = lax.scan(step_fn, start, grouped)
    token_grad = outs[0].reshape(TOKENS, D)
    combine_grad = outs[1].reshape(TOKENS, 2)
    return token_grad, combine_grad, sums[0], sums[1]
```

```python
import jax
import jax.numpy as jnp
from jax import lax
from jax.experimental import pallas as pl
from jax.experimental.pallas import tpu as pltpu
from jax.sharding import PartitionSpec as P

MESH = pl.DeviceIdType.MESH
BF16 = jnp.bfloat16
F32 = jnp.float32

D = 1024
FF = 1024
TOK = 256
CAP = 32
EXPERTS = 32
LOCAL = 2
PEERS = 16
SLOTS = PEERS * CAP
WIDE = 2 * FF + FF
HALF = 128
TILE = 256
RET = D + 128
STAGE = 128

PARTNERS = (
    (0, 0), (1, 0), (3, 0), (0, 1), (0, 3), (1, 1), (3, 3), (2, 2),
    (1, 3), (3, 1), (2, 0), (0, 2), (1, 2), (3, 2), (2, 1), (2, 3),
)
STEPS = (2, 1, 3, 0)


def dot(a, b):
    return lax.dot_general(a, b, (((1,), (0,)), ((), ())), preferred_element_type=F32)


def dot_nt(a, b):
    return lax.dot_general(a, b, (((1,), (1,)), ((), ())), preferred_element_type=F32)


def dot_tn(a, b):
    return lax.dot_general(a, b, (((0,), (0,)), ((), ())), preferred_element_type=F32)


def kernel(
    tokens, cotangent, combine, ids, capacity, w_in, w_down,
    token_out, combine_out, inner_out, down_out,
    raw_in, raw_down, win, wdown, pick0, pick1, send, recv, hidden, dpre, turned,
    part, core_sum, relay, arrived, ret_send, ret_recv,
    raw_sem, send_sem, recv_sem, ret_send_sem, ret_recv_sem,
    core_send_sem, core_recv_sem, z_send_sem, z_recv_sem,
):
    dp = lax.axis_index("dp")
    ex = lax.axis_index("expert")
    z, core = dp // 2, dp % 2
    y, x = ex // 4, ex % 4

    def partner(i, sign):
        dx, dy = PARTNERS[i]
        return ((y + 4 + sign * dy) % 4) * 4 + (x + 4 + sign * dx) % 4

    def along_z(step):
        return (((z + step) % 4) * 2 + core, ex)

    sibling = (z * 2 + 1 - core, ex)

    def dispatch(e, i):
        return pltpu.make_async_remote_copy(
            src_ref=send.at[e, i], dst_ref=recv.at[e, i],
            send_sem=send_sem.at[e, i], recv_sem=recv_sem.at[e, i],
            device_id=(dp, partner(i, 1)), device_id_type=MESH,
        )

    def give_back(e, i):
        return pltpu.make_async_remote_copy(
            src_ref=ret_send.at[e, i], dst_ref=ret_recv.at[e, i],
            send_sem=ret_send_sem.at[e, i], recv_sem=ret_recv_sem.at[e, i],
            device_id=(dp, partner(i, -1)), device_id_type=MESH,
        )

    def to_sibling(e, s):
        return pltpu.make_async_remote_copy(
            src_ref=part.at[s, 1 - core], dst_ref=core_sum.at[e, s],
            send_sem=core_send_sem.at[e, s], recv_sem=core_recv_sem.at[e, s],
            device_id=sibling, device_id_type=MESH,
        )

    half = HALF // 2

    def z_copy(e, k):
        src, dst, step = (
            (core_sum.at[e, 0, pl.ds(0, half)], relay.at[e, 0], 1),
            (core_sum.at[e, 0, pl.ds(half, half)], relay.at[e, 1], 3),
            (core_sum.at[e, 1, pl.ds(half, half)], arrived.at[e, 0, pl.ds(half, half)], 1),
            (core_sum.at[e, 2, pl.ds(0, half)], arrived.at[e, 1, pl.ds(0, half)], 3),
            (core_sum.at[e, 1, pl.ds(0, half)], arrived.at[e, 0, pl.ds(0, half)], 1),
            (core_sum.at[e, 2, pl.ds(half, half)], arrived.at[e, 1, pl.ds(half, half)], 3),
        )[k]
        return pltpu.make_async_remote_copy(
            src_ref=src, dst_ref=dst, send_sem=z_send_sem.at[e, k], recv_sem=z_recv_sem.at[e, k],
            device_id=along_z(step), device_id_type=MESH,
        )

    def raw_copy(j, slot, which):
        src, dst = ((w_in, raw_in), (w_down, raw_down))[which]
        return pltpu.make_async_copy(
            src.at[pl.ds(pl.multiple_of(j * STAGE, STAGE), STAGE)], dst.at[slot],
            raw_sem.at[which, slot],
        )

    for which in (0, 1):
        raw_copy(0, 0, which).start()

    barrier = pltpu.get_barrier_semaphore()
    greeted = [(dp, partner(i, 1)) for i in range(1, PEERS)] + [sibling, along_z(1), along_z(3)]
    for device in greeted:
        pl.semaphore_signal(barrier, inc=1, device_id=device, device_id_type=MESH)

    rows = lax.broadcasted_iota(jnp.int32, (TOK, TOK), 0)
    columns = lax.broadcasted_iota(jnp.int32, (TOK, TOK), 1)
    earlier = (columns < rows).astype(F32).astype(BF16)
    lane = lax.broadcasted_iota(jnp.int32, (TOK, EXPERTS), 1)
    id0, id1 = ids[:, 0:1], ids[:, 1:2]
    named0 = (id0 == lane).astype(F32)
    named1 = (id1 == lane).astype(F32)
    before = dot(earlier, (named0 + named1).astype(BF16))
    limits = capacity[...].astype(F32)

    def target(named, number):
        position = jnp.sum(named * before, axis=1, keepdims=True)
        limit = jnp.sum(named * limits, axis=1, keepdims=True)
        return jnp.where(position < limit, number * CAP + position.astype(jnp.int32), -1)

    target0, target1 = target(named0, id0), target(named1, id1)
    slot_lane = lax.broadcasted_iota(jnp.int32, (1, SLOTS), 1)
    first = jnp.zeros((1, SLOTS), jnp.int32)
    for i in range(PEERS):
        first = jnp.where(slot_lane // CAP == i, partner(i, 1) * (LOCAL * CAP), first)
    first = first + slot_lane % CAP
    for e in range(LOCAL):
        wanted = first + e * CAP
        pick0[e] = (target0 == wanted).astype(F32).astype(BF16)
        pick1[e] = (target1 == wanted).astype(F32).astype(BF16)

    cb0 = combine[:, 0:1].astype(BF16).astype(F32)
    cb1 = combine[:, 1:2].astype(BF16).astype(F32)

    def gather(e, group):
        lanes = pl.ds(group * 128, 128)
        p0, p1 = pick0[e, :, lanes], pick1[e, :, lanes]
        for c in range(0, D, TILE):
            cols = pl.ds(c, TILE)
            cot = cotangent[:, cols].astype(F32)
            rows_x = dot_tn(p0 + p1, tokens[:, cols]).astype(BF16)
            rows_s = (
                dot_tn(p0, (cb0 * cot).astype(BF16)) + dot_tn(p1, (cb1 * cot).astype(BF16))
            ).astype(BF16)
            for j in range(4):
                i = group * 4 + j
                buffer = recv if i == 0 else send
                buffer[e, i, 0:CAP, cols] = rows_x[j * CAP:(j + 1) * CAP]
                buffer[e, i, CAP:2 * CAP, cols] = rows_s[j * CAP:(j + 1) * CAP]

    def start_dispatch(e, lo, hi):
        for i in range(max(lo, 1), hi):
            dispatch(e, i).start()

    for group in range(4):
        gather(0, group)
        if group == 0:
            pl.semaphore_wait(barrier, len(greeted))
        start_dispatch(0, group * 4, group * 4 + 4)
    for group in range(4):
        gather(1, group)

    def settle(j, _):
        slot = j % 2

        @pl.when(j + 1 < D // STAGE)
        def _():
            for which in (0, 1):
                raw_copy(j + 1, 1 - slot, which).start()

        for which in (0, 1):
            raw_copy(j, slot, which).wait()

        def block(b, _):
            src = pl.multiple_of(b * 16, 16)
            dst = pl.ds(pl.multiple_of(j * STAGE + b * 16, 16), 16)
            win[:, dst, :] = jnp.swapaxes(raw_in[slot, pl.ds(src, 16)], 0, 1)
            wdown[:, dst, :] = jnp.swapaxes(raw_down[slot, pl.ds(src, 16)], 0, 1)
            return 0

        lax.fori_loop(0, STAGE // 16, block, 0)
        return 0

    lax.fori_loop(0, D // STAGE, settle, 0)

    def arrive(e, lo, hi):
        for i in range(max(lo, 1), hi):
            dispatch(e, i).wait_recv()

    def rows_of(e, h, lo, cols):
        return recv[e, h * 8:h * 8 + 8, lo:lo + CAP, cols].reshape(8 * CAP, -1)

    def forward(e, h):
        here = pl.ds(h * 256, 256)

        def tile(n, total):
            at = pl.multiple_of(n * TILE, TILE)
            cols, upper = pl.ds(at, TILE), pl.ds(FF + at, TILE)
            xs = rows_of(e, h, 0, slice(None))
            gate = dot(xs, win[e, :, cols])
            up = dot(xs, win[e, :, upper])
            dh = dot_nt(rows_of(e, h, CAP, slice(None)), wdown[e, cols, :])
            sig = jax.nn.sigmoid(gate)
            act = gate * sig
            hid = (act * up).astype(BF16)
            hidden[here, cols] = hid
            dpre[here, cols] = (dh * up * sig * (1.0 + gate * (1.0 - sig))).astype(BF16)
            dpre[here, upper] = (dh * act).astype(BF16)
            return total + jnp.sum(hid.astype(F32) * dh, axis=1, keepdims=True)

        total = lax.fori_loop(0, FF // TILE, tile, jnp.zeros((256, 1), F32))
        total = jnp.broadcast_to(total.astype(BF16), (256, 128)).reshape(8, CAP, 128)
        for j in range(8):
            i = h * 8 + j
            buffer = ret_recv if i == 0 else ret_send
            buffer[e, i, :, D:RET] = total[j]

    def partial(e, s):
        at = pl.multiple_of(((z + STEPS[s]) % 4) * TILE, TILE)
        turned[...] = recv[e, :, 0:CAP, pl.ds(at, TILE)].reshape(SLOTS, TILE).T

        def inner_tile(n, _):
            cols = pl.ds(pl.multiple_of(n * TILE, TILE), TILE)
            part[s, :, :, cols] = dot(turned[...], dpre[:, cols]).astype(BF16).reshape(2, HALF, TILE)
            return 0

        lax.fori_loop(0, 2 * FF // TILE, inner_tile, 0)
        turned[...] = hidden[:, pl.ds(at, TILE)].T

        def down_tile(n, _):
            at = pl.multiple_of(n * TILE, TILE)
            scaled = recv[e, :, CAP:2 * CAP, pl.ds(at, TILE)].reshape(SLOTS, TILE)
            part[s, :, :, pl.ds(2 * FF + at, TILE)] = (
                dot(turned[...], scaled).astype(BF16).reshape(2, HALF, TILE)
            )
            return 0

        lax.fori_loop(0, D // TILE, down_tile, 0)

    def add_rows(dst, lo, count, other):
        def block(b, _):
            at = pl.multiple_of(b * 16, 16)
            here = dst[pl.ds(lo + at, 16)].astype(F32)
            dst[pl.ds(lo + at, 16)] = (here + other[pl.ds(at, 16)].astype(F32)).astype(BF16)
            return 0

        lax.fori_loop(0, count // 16, block, 0)

    def meet_sibling(e, s):
        to_sibling(e, s).wait_recv()
        add_rows(core_sum.at[e, s], 0, HALF, part.at[s, core])
        for k in ((0, 1), (2,), (3,), ())[s]:
            z_copy(e, k).start()

    def weight_sums(e):
        for s in range(4):
            partial(e, s)
            to_sibling(e, s).start()
            if s > 0:
                meet_sibling(e, s - 1)
        meet_sibling(e, 3)

    def pass_on(e):
        z_copy(e, 0).wait_recv()
        add_rows(core_sum.at[e, 1], 0, half, relay.at[e, 0])
        z_copy(e, 4).start()
        z_copy(e, 1).wait_recv()
        add_rows(core_sum.at[e, 2], half, half, relay.at[e, 1])
        z_copy(e, 5).start()

    def input_grad(e, h):
        def tile(n, _):
            cols = pl.ds(pl.multiple_of(n * TILE, TILE), TILE)
            grad = dot_nt(dpre[pl.ds(h * 256, 256), :], win[e, cols, :]).astype(BF16)
            grad = grad.reshape(8, CAP, TILE)
            for j in range(8):
                i = h * 8 + j
                buffer = ret_recv if i == 0 else ret_send
                buffer[e, i, :, cols] = grad[j]
            return 0

        lax.fori_loop(0, D // TILE, tile, 0)
        for i in range(max(h * 8, 1), h * 8 + 8):
            give_back(e, i).start()

    def finish_sums(e):
        for k in (2, 3, 4, 5):
            z_copy(e, k).wait_recv()

        def block(b, _):
            at = pl.ds(pl.multiple_of(b * 16, 16), 16)
            total = core_sum[e, 3, at].astype(F32)
            total = total + arrived[e, 0, at].astype(F32) + arrived[e, 1, at].astype(F32)
            inner_out[e, at, :] = total[:, :2 * FF]
            down_out[e, at, :] = total[:, 2 * FF:]
            return 0

        lax.fori_loop(0, HALF // 16, block, 0)

    for e in range(LOCAL):
        arrive(e, 0, 8)
        if e == 0:
            start_dispatch(1, 0, PEERS)
        forward(e, 0)
        arrive(e, 8, PEERS)
        forward(e, 1)
        if e == 1:
            for s in range(4):
                to_sibling(0, s).wait_send()
        weight_sums(e)
        input_grad(e, 0)
        pass_on(e)
        input_grad(e, 1)

    finish_sums(0)

    for e in range(LOCAL):
        for i in range(1, PEERS):
            give_back(e, i).wait_recv()
    for c in range(0, D, TILE):
        cols = pl.ds(c, TILE)
        total = jnp.zeros((TOK, TILE), F32)
        for e in range(LOCAL):
            total = total + dot(
                pick0[e] + pick1[e], ret_recv[e, :, :, cols].reshape(SLOTS, TILE)
            )
        token_out[:, cols] = total.astype(BF16)
    for k, (pick, cb) in enumerate(((pick0, cb0), (pick1, cb1))):
        total = jnp.zeros((TOK, 128), F32)
        for e in range(LOCAL):
            total = total + dot(pick[e], ret_recv[e, :, :, D:RET].reshape(SLOTS, 128))
        combine_out[:, k:k + 1] = (total[:, 0:1] / cb).astype(BF16)

    finish_sums(1)

    for e in range(LOCAL):
        for i in range(1, PEERS):
            dispatch(e, i).wait_send()
            give_back(e, i).wait_send()
        for k in range(6):
            z_copy(e, k).wait_send()
    for s in range(4):
        to_sibling(1, s).wait_send()


def on_device(tokens, cotangent, combine, expert_ids, capacity, weight_in, weight_down):
    vmem = pl.BlockSpec(memory_space=pltpu.VMEM)
    hbm = pl.BlockSpec(memory_space=pl.ANY)
    token_grad, combine_grad, inner, down = pl.pallas_call(
        kernel,
        out_shape=(
            jax.ShapeDtypeStruct((TOK, D), BF16),
            jax.ShapeDtypeStruct((TOK, 2), BF16),
            jax.ShapeDtypeStruct((LOCAL, HALF, 2 * FF), F32),
            jax.ShapeDtypeStruct((LOCAL, HALF, D), F32),
        ),
        in_specs=[vmem] * 5 + [hbm] * 2,
        out_specs=(vmem,) * 4,
        scratch_shapes=[
            pltpu.VMEM((2, STAGE, LOCAL, 2 * FF), BF16),
            pltpu.VMEM((2, STAGE, LOCAL, D), BF16),
            pltpu.VMEM((LOCAL, D, 2 * FF), BF16),
            pltpu.VMEM((LOCAL, FF, D), BF16),
            pltpu.VMEM((LOCAL, TOK, SLOTS), BF16),
            pltpu.VMEM((LOCAL, TOK, SLOTS), BF16),
            pltpu.VMEM((LOCAL, PEERS, 2 * CAP, D), BF16),
            pltpu.VMEM((LOCAL, PEERS, 2 * CAP, D), BF16),
            pltpu.VMEM((SLOTS, FF), BF16),
            pltpu.VMEM((SLOTS, 2 * FF), BF16),
            pltpu.VMEM((TILE, SLOTS), BF16),
            pltpu.VMEM((4, 2, HALF, WIDE), BF16),
            pltpu.VMEM((LOCAL, 4, HALF, WIDE), BF16),
            pltpu.VMEM((LOCAL, 2, HALF // 2, WIDE), BF16),
            pltpu.VMEM((LOCAL, 2, HALF, WIDE), BF16),
            pltpu.VMEM((LOCAL, PEERS, CAP, RET), BF16),
            pltpu.VMEM((LOCAL, PEERS, CAP, RET), BF16),
            pltpu.SemaphoreType.DMA((2, 2)),
            pltpu.SemaphoreType.DMA((LOCAL, PEERS)),
            pltpu.SemaphoreType.DMA((LOCAL, PEERS)),
            pltpu.SemaphoreType.DMA((LOCAL, PEERS)),
            pltpu.SemaphoreType.DMA((LOCAL, PEERS)),
            pltpu.SemaphoreType.DMA((LOCAL, 4)),
            pltpu.SemaphoreType.DMA((LOCAL, 4)),
            pltpu.SemaphoreType.DMA((LOCAL, 6)),
            pltpu.SemaphoreType.DMA((LOCAL, 6)),
        ],
        compiler_params=pltpu.CompilerParams(
            collective_id=0, has_side_effects=True, vmem_limit_bytes=62 * 2**20
        ),
        name="moe_backward",
    )(tokens, cotangent, combine, expert_ids, capacity.reshape(1, EXPERTS), weight_in, weight_down)
    return (
        token_grad,
        combine_grad,
        jnp.transpose(inner, (1, 0, 2)),
        jnp.transpose(down, (1, 0, 2)),
    )


def solution(mesh):
    placed = (
        P(("dp", "expert"), None),
        P(("dp", "expert"), None),
        P(("dp", "expert"), None),
        P(("dp", "expert"), None),
        P(),
        P(None, "expert", None),
        P(None, "expert", None),
    )
    return jax.shard_map(
        on_device,
        mesh=mesh,
        in_specs=placed,
        out_specs=(
            P(("dp", "expert"), None),
            P(("dp", "expert"), None),
            P("dp", "expert", None),
            P("dp", "expert", None),
        ),
        check_vma=False,
    )
```

```python
import jax
import jax.numpy as jnp
from jax import lax
from jax.experimental import pallas as pl
from jax.experimental.pallas import tpu as pltpu
from jax.sharding import PartitionSpec as P

MESH = pl.DeviceIdType.MESH
BF16 = jnp.bfloat16
F32 = jnp.float32

D = 1024
FF = 1024
TOK = 256
CAP = 32
EXPERTS = 32
LOCAL = 2
PEERS = 16
SLOTS = PEERS * CAP
WIDE = 2 * FF + FF
HALF = 128
TILE = 256
RET = D + 128
STAGE = 128
PARTS = 4

PARTNERS = (
    (0, 0), (1, 0), (3, 0), (0, 1), (0, 3), (1, 1), (3, 3), (2, 2),
    (1, 3), (3, 1), (2, 0), (0, 2), (1, 2), (3, 2), (2, 1), (2, 3),
)
STEPS = (2, 1, 3, 0)


def dot(a, b):
    return lax.dot_general(a, b, (((1,), (0,)), ((), ())), preferred_element_type=F32)


def dot_nt(a, b):
    return lax.dot_general(a, b, (((1,), (1,)), ((), ())), preferred_element_type=F32)


def dot_tn(a, b):
    return lax.dot_general(a, b, (((0,), (0,)), ((), ())), preferred_element_type=F32)


def kernel(
    tokens_in, cotangent_in, combine_in, ids_in, capacity_in, w_in, w_down,
    token_out, combine_out, own, arrived,
    tokens, cotangent, combine, ids, capacity,
    raw_in, raw_down, win, wdown, pick0, pick1, send, recv, hidden, dpre, turned,
    part, core_sum, relay, ret_send, ret_recv,
    in_sem, raw_sem, send_sem, recv_sem, ret_send_sem, ret_recv_sem,
    core_send_sem, core_recv_sem, z_send_sem, z_recv_sem, keep_sem,
):
    dp = lax.axis_index("dp")
    ex = lax.axis_index("expert")
    z, core = dp // 2, dp % 2
    y, x = ex // 4, ex % 4

    def partner(i, sign):
        dx, dy = PARTNERS[i]
        return ((y + 4 + sign * dy) % 4) * 4 + (x + 4 + sign * dx) % 4

    def along_z(step):
        return (((z + step) % 4) * 2 + core, ex)

    sibling = (z * 2 + 1 - core, ex)

    def dispatch(e, i):
        return pltpu.make_async_remote_copy(
            src_ref=send.at[e, i], dst_ref=recv.at[e, i],
            send_sem=send_sem.at[e, i], recv_sem=recv_sem.at[e, i],
            device_id=(dp, partner(i, 1)), device_id_type=MESH,
        )

    def give_back(e, i):
        return pltpu.make_async_remote_copy(
            src_ref=ret_send.at[e, i], dst_ref=ret_recv.at[e, i],
            send_sem=ret_send_sem.at[e, i], recv_sem=ret_recv_sem.at[e, i],
            device_id=(dp, partner(i, -1)), device_id_type=MESH,
        )

    def to_sibling(e, s):
        return pltpu.make_async_remote_copy(
            src_ref=part.at[s, 1 - core], dst_ref=core_sum.at[e, s],
            send_sem=core_send_sem.at[e, s], recv_sem=core_recv_sem.at[e, s],
            device_id=sibling, device_id_type=MESH,
        )

    half = HALF // 2

    def z_copy(e, k):
        src, dst, step = (
            (core_sum.at[e, 0, pl.ds(0, half)], relay.at[e, 0], 1),
            (core_sum.at[e, 0, pl.ds(half, half)], relay.at[e, 1], 3),
            (core_sum.at[e, 1, pl.ds(half, half)], arrived.at[e, 0, pl.ds(half, half)], 1),
            (core_sum.at[e, 2, pl.ds(0, half)], arrived.at[e, 1, pl.ds(0, half)], 3),
            (core_sum.at[e, 1, pl.ds(0, half)], arrived.at[e, 0, pl.ds(0, half)], 1),
            (core_sum.at[e, 2, pl.ds(half, half)], arrived.at[e, 1, pl.ds(half, half)], 3),
        )[k]
        return pltpu.make_async_remote_copy(
            src_ref=src, dst_ref=dst, send_sem=z_send_sem.at[e, k], recv_sem=z_recv_sem.at[e, k],
            device_id=along_z(step), device_id_type=MESH,
        )

    def keep(e):
        return pltpu.make_async_copy(core_sum.at[e, 3], own.at[e], keep_sem.at[e])

    def raw_copy(j, slot, which):
        src, dst = ((w_in, raw_in), (w_down, raw_down))[which]
        return pltpu.make_async_copy(
            src.at[pl.ds(pl.multiple_of(j * STAGE, STAGE), STAGE)], dst.at[slot],
            raw_sem.at[which, slot],
        )

    barrier = pltpu.get_barrier_semaphore()
    greeted = [(dp, partner(i, 1)) for i in range(1, PEERS)] + [sibling, along_z(1), along_z(3)]
    for device in greeted:
        pl.semaphore_signal(barrier, inc=1, device_id=device, device_id_type=MESH)

    fetched = [
        pltpu.make_async_copy(src, dst, in_sem.at[n])
        for n, (src, dst) in enumerate((
            (ids_in, ids), (capacity_in, capacity), (combine_in, combine),
            (tokens_in, tokens), (cotangent_in, cotangent),
        ))
    ]
    for copy in fetched:
        copy.start()
    for which in (0, 1):
        raw_copy(0, 0, which).start()
    for copy in fetched[:3]:
        copy.wait()

    rows = lax.broadcasted_iota(jnp.int32, (TOK, TOK), 0)
    columns = lax.broadcasted_iota(jnp.int32, (TOK, TOK), 1)
    earlier = (columns < rows).astype(F32).astype(BF16)
    lane = lax.broadcasted_iota(jnp.int32, (TOK, EXPERTS), 1)
    stood = jnp.concatenate(
        [ids[...].astype(F32), combine[...].astype(BF16).astype(F32), jnp.zeros((4, TOK), F32)], axis=0
    ).T
    id0, id1 = stood[:, 0:1].astype(jnp.int32), stood[:, 1:2].astype(jnp.int32)
    cb0, cb1 = stood[:, 2:3], stood[:, 3:4]
    named0 = (id0 == lane).astype(F32)
    named1 = (id1 == lane).astype(F32)
    before = dot(earlier, (named0 + named1).astype(BF16))
    limits = capacity[...].astype(F32)

    def target(named, number):
        position = jnp.sum(named * before, axis=1, keepdims=True)
        limit = jnp.sum(named * limits, axis=1, keepdims=True)
        return jnp.where(position < limit, number * CAP + position.astype(jnp.int32), -1)

    target0, target1 = target(named0, id0), target(named1, id1)
    slot_lane = lax.broadcasted_iota(jnp.int32, (1, SLOTS), 1)
    first = jnp.zeros((1, SLOTS), jnp.int32)
    for i in range(PEERS):
        first = jnp.where(slot_lane // CAP == i, partner(i, 1) * (LOCAL * CAP), first)
    first = first + slot_lane % CAP
    for e in range(LOCAL):
        wanted = first + e * CAP
        pick0[e] = (target0 == wanted).astype(F32).astype(BF16)
        pick1[e] = (target1 == wanted).astype(F32).astype(BF16)

    def gather(e, group):
        lanes = pl.ds(group * 128, 128)
        p0, p1 = pick0[e, :, lanes], pick1[e, :, lanes]
        for c in range(0, D, TILE):
            cols = pl.ds(c, TILE)
            cot = cotangent[:, cols].astype(F32)
            rows_x = dot_tn(p0 + p1, tokens[:, cols]).astype(BF16)
            rows_s = (
                dot_tn(p0, (cb0 * cot).astype(BF16)) + dot_tn(p1, (cb1 * cot).astype(BF16))
            ).astype(BF16)
            for j in range(4):
                i = group * 4 + j
                buffer = recv if i == 0 else send
                buffer[e, i, 0:CAP, cols] = rows_x[j * CAP:(j + 1) * CAP]
                buffer[e, i, CAP:2 * CAP, cols] = rows_s[j * CAP:(j + 1) * CAP]

    def start_dispatch(e, lo, hi):
        for i in range(max(lo, 1), hi):
            dispatch(e, i).start()

    for copy in fetched[3:]:
        copy.wait()
    for group in range(4):
        gather(0, group)
        if group == 0:
            pl.semaphore_wait(barrier, len(greeted))
        start_dispatch(0, group * 4, group * 4 + 4)
    for group in range(4):
        gather(1, group)

    def settle(j, _):
        slot = j % 2

        @pl.when(j + 1 < D // STAGE)
        def _():
            for which in (0, 1):
                raw_copy(j + 1, 1 - slot, which).start()

        for which in (0, 1):
            raw_copy(j, slot, which).wait()

        def block(b, _):
            src = pl.multiple_of(b * 16, 16)
            dst = pl.ds(pl.multiple_of(j * STAGE + b * 16, 16), 16)
            win[:, dst, :] = jnp.swapaxes(raw_in[slot, pl.ds(src, 16)], 0, 1)
            wdown[:, dst, :] = jnp.swapaxes(raw_down[slot, pl.ds(src, 16)], 0, 1)
            return 0

        lax.fori_loop(0, STAGE // 16, block, 0)
        return 0

    lax.fori_loop(0, D // STAGE, settle, 0)

    def arrive(e, lo, hi):
        for i in range(max(lo, 1), hi):
            dispatch(e, i).wait_recv()

    def rows_of(e, h, lo, cols):
        return recv[e, h * 8:h * 8 + 8, lo:lo + CAP, cols].reshape(8 * CAP, -1)

    def forward(e, h):
        here = pl.ds(h * 256, 256)

        def tile(n, total):
            at = pl.multiple_of(n * TILE, TILE)
            cols, upper = pl.ds(at, TILE), pl.ds(FF + at, TILE)
            xs = rows_of(e, h, 0, slice(None))
            gate = dot(xs, win[e, :, cols])
            up = dot(xs, win[e, :, upper])
            dh = dot_nt(rows_of(e, h, CAP, slice(None)), wdown[e, cols, :])
            sig = jax.nn.sigmoid(gate)
            act = gate * sig
            hid = (act * up).astype(BF16)
            hidden[here, cols] = hid
            dpre[here, cols] = (dh * up * sig * (1.0 + gate * (1.0 - sig))).astype(BF16)
            dpre[here, upper] = (dh * act).astype(BF16)
            return total + jnp.sum(hid.astype(F32) * dh, axis=1, keepdims=True)

        total = lax.fori_loop(0, FF // TILE, tile, jnp.zeros((256, 1), F32), unroll=True)
        total = jnp.broadcast_to(total.astype(BF16), (256, 128)).reshape(8, CAP, 128)
        for j in range(8):
            i = h * 8 + j
            buffer = ret_recv if i == 0 else ret_send
            buffer[e, i, :, D:RET] = total[j]

    def partial(e, s):
        at = pl.multiple_of(((z + STEPS[s]) % 4) * TILE, TILE)
        turned[...] = recv[e, :, 0:CAP, pl.ds(at, TILE)].reshape(SLOTS, TILE).T

        def inner_tile(n, _):
            cols = pl.ds(pl.multiple_of(n * TILE, TILE), TILE)
            part[s, :, :, cols] = dot(turned[...], dpre[:, cols]).astype(BF16).reshape(2, HALF, TILE)
            return 0

        lax.fori_loop(0, 2 * FF // TILE, inner_tile, 0, unroll=True)
        turned[...] = hidden[:, pl.ds(at, TILE)].T

        def down_tile(n, _):
            at = pl.multiple_of(n * TILE, TILE)
            scaled = recv[e, :, CAP:2 * CAP, pl.ds(at, TILE)].reshape(SLOTS, TILE)
            part[s, :, :, pl.ds(2 * FF + at, TILE)] = (
                dot(turned[...], scaled).astype(BF16).reshape(2, HALF, TILE)
            )
            return 0

        lax.fori_loop(0, D // TILE, down_tile, 0, unroll=True)

    def add_rows(dst, lo, count, other):
        def block(b, _):
            at = pl.multiple_of(b * 16, 16)
            here = dst[pl.ds(lo + at, 16)].astype(F32)
            dst[pl.ds(lo + at, 16)] = (here + other[pl.ds(at, 16)].astype(F32)).astype(BF16)
            return 0

        lax.fori_loop(0, count // 16, block, 0)

    def meet_sibling(e, s):
        to_sibling(e, s).wait_recv()
        add_rows(core_sum.at[e, s], 0, HALF, part.at[s, core])
        for k in ((0, 1), (2,), (3,), ())[s]:
            z_copy(e, k).start()

    def weight_sums(e):
        for s in range(4):
            partial(e, s)
            to_sibling(e, s).start()
            if s > 0:
                meet_sibling(e, s - 1)
        meet_sibling(e, 3)
        keep(e).start()

    def pass_on(e):
        z_copy(e, 0).wait_recv()
        add_rows(core_sum.at[e, 1], 0, half, relay.at[e, 0])
        z_copy(e, 4).start()
        z_copy(e, 1).wait_recv()
        add_rows(core_sum.at[e, 2], half, half, relay.at[e, 1])
        z_copy(e, 5).start()

    def input_grad(e, h):
        def tile(n, _):
            cols = pl.ds(pl.multiple_of(n * TILE, TILE), TILE)
            grad = dot_nt(dpre[pl.ds(h * 256, 256), :], win[e, cols, :]).astype(BF16)
            grad = grad.reshape(8, CAP, TILE)
            for j in range(8):
                i = h * 8 + j
                buffer = ret_recv if i == 0 else ret_send
                buffer[e, i, :, cols] = grad[j]
            return 0

        lax.fori_loop(0, D // TILE, tile, 0, unroll=True)
        for i in range(max(h * 8, 1), h * 8 + 8):
            give_back(e, i).start()

    for e in range(LOCAL):
        arrive(e, 0, 8)
        if e == 0:
            start_dispatch(1, 0, PEERS)
        forward(e, 0)
        arrive(e, 8, PEERS)
        forward(e, 1)
        if e == 1:
            for s in range(4):
                to_sibling(0, s).wait_send()
        weight_sums(e)
        input_grad(e, 0)
        pass_on(e)
        input_grad(e, 1)

    for e in range(LOCAL):
        for i in range(1, PEERS):
            give_back(e, i).wait_recv()
    for c in range(0, D, TILE):
        cols = pl.ds(c, TILE)
        total = jnp.zeros((TOK, TILE), F32)
        for e in range(LOCAL):
            total = total + dot(
                pick0[e] + pick1[e], ret_recv[e, :, :, cols].reshape(SLOTS, TILE)
            )
        token_out[:, cols] = total.astype(BF16)
    router = []
    for pick, cb in ((pick0, cb0), (pick1, cb1)):
        total = jnp.zeros((TOK, 128), F32)
        for e in range(LOCAL):
            total = total + dot(pick[e], ret_recv[e, :, :, D:RET].reshape(SLOTS, 128))
        router.append(total[:, 0:1] / cb)
    router = jnp.concatenate(router + [jnp.zeros((TOK, 6), F32)], axis=1)
    combine_out[...] = router.T[0:2].astype(BF16)

    for e in range(LOCAL):
        for i in range(1, PEERS):
            dispatch(e, i).wait_send()
            give_back(e, i).wait_send()
        for k in range(6):
            z_copy(e, k).wait_send()
        for k in (2, 3, 4, 5):
            z_copy(e, k).wait_recv()
        keep(e).wait()
    for s in range(4):
        to_sibling(1, s).wait_send()


def finish(
    token_in, combine_in, own_in, arrived_in, token_out, combine_out, inner_out, down_out,
    token, own, arrived, inner, down, token_sem, in_sem, out_sem,
):
    rows = HALF // PARTS
    fetched = pltpu.make_async_copy(token_in, token, token_sem.at[0])
    passed = pltpu.make_async_copy(token, token_out, token_sem.at[1])
    fetched.start()

    def load(p):
        here = pl.ds(p * rows, rows)
        return (
            pltpu.make_async_copy(own_in.at[:, here], own.at[:, here], in_sem.at[0, p]),
            pltpu.make_async_copy(arrived_in.at[:, :, here], arrived.at[:, :, here], in_sem.at[1, p]),
        )

    def store(p):
        here = pl.ds(p * rows, rows)
        return (
            pltpu.make_async_copy(inner.at[here], inner_out.at[here], out_sem.at[0, p]),
            pltpu.make_async_copy(down.at[here], down_out.at[here], out_sem.at[1, p]),
        )

    for p in range(PARTS):
        for copy in load(p):
            copy.start()
    combine_out[...] = combine_in[...]
    fetched.wait()
    passed.start()
    for p in range(PARTS):
        for copy in load(p):
            copy.wait()

        def block(b, _):
            at = pl.ds(pl.multiple_of(p * rows + b * 16, 16), 16)
            total = own[:, at].astype(F32)
            total = total + arrived[:, 0, at].astype(F32) + arrived[:, 1, at].astype(F32)
            total = jnp.swapaxes(total, 0, 1)
            inner[at] = total[..., :2 * FF]
            down[at] = total[..., 2 * FF:]
            return 0

        lax.fori_loop(0, rows // 16, block, 0)
        for copy in store(p):
            copy.start()
    passed.wait()
    for p in range(PARTS):
        for copy in store(p):
            copy.wait()


def on_device(tokens, cotangent, combine, expert_ids, capacity, weight_in, weight_down):
    vmem = pl.BlockSpec(memory_space=pltpu.VMEM)
    hbm = pl.BlockSpec(memory_space=pl.ANY)
    token_grad, combine_grad, own, arrived = pl.pallas_call(
        kernel,
        out_shape=(
            jax.ShapeDtypeStruct((TOK, D), BF16),
            jax.ShapeDtypeStruct((2, TOK), BF16),
            jax.ShapeDtypeStruct((LOCAL, HALF, WIDE), BF16),
            jax.ShapeDtypeStruct((LOCAL, 2, HALF, WIDE), BF16),
        ),
        in_specs=[hbm] * 7,
        out_specs=(vmem, vmem, hbm, hbm),
        scratch_shapes=[
            pltpu.VMEM((TOK, D), BF16),
            pltpu.VMEM((TOK, D), BF16),
            pltpu.VMEM((2, TOK), F32),
            pltpu.VMEM((2, TOK), jnp.int32),
            pltpu.VMEM((1, EXPERTS), jnp.int32),
            pltpu.VMEM((2, STAGE, LOCAL, 2 * FF), BF16),
            pltpu.VMEM((2, STAGE, LOCAL, D), BF16),
            pltpu.VMEM((LOCAL, D, 2 * FF), BF16),
            pltpu.VMEM((LOCAL, FF, D), BF16),
            pltpu.VMEM((LOCAL, TOK, SLOTS), BF16),
            pltpu.VMEM((LOCAL, TOK, SLOTS), BF16),
            pltpu.VMEM((LOCAL, PEERS, 2 * CAP, D), BF16),
            pltpu.VMEM((LOCAL, PEERS, 2 * CAP, D), BF16),
            pltpu.VMEM((SLOTS, FF), BF16),
            pltpu.VMEM((SLOTS, 2 * FF), BF16),
            pltpu.VMEM((TILE, SLOTS), BF16),
            pltpu.VMEM((4, 2, HALF, WIDE), BF16),
            pltpu.VMEM((LOCAL, 4, HALF, WIDE), BF16),
            pltpu.VMEM((LOCAL, 2, HALF // 2, WIDE), BF16),
            pltpu.VMEM((LOCAL, PEERS, CAP, RET), BF16),
            pltpu.VMEM((LOCAL, PEERS, CAP, RET), BF16),
            pltpu.SemaphoreType.DMA((5,)),
            pltpu.SemaphoreType.DMA((2, 2)),
            pltpu.SemaphoreType.DMA((LOCAL, PEERS)),
            pltpu.SemaphoreType.DMA((LOCAL, PEERS)),
            pltpu.SemaphoreType.DMA((LOCAL, PEERS)),
            pltpu.SemaphoreType.DMA((LOCAL, PEERS)),
            pltpu.SemaphoreType.DMA((LOCAL, 4)),
            pltpu.SemaphoreType.DMA((LOCAL, 4)),
            pltpu.SemaphoreType.DMA((LOCAL, 6)),
            pltpu.SemaphoreType.DMA((LOCAL, 6)),
            pltpu.SemaphoreType.DMA((LOCAL,)),
        ],
        compiler_params=pltpu.CompilerParams(
            collective_id=0, has_side_effects=True, vmem_limit_bytes=62 * 2**20
        ),
        name="moe_backward",
    )(
        tokens, cotangent, combine.T, expert_ids.T, capacity.reshape(1, EXPERTS),
        weight_in, weight_down,
    )
    token_grad, combine_grad, inner, down = pl.pallas_call(
        finish,
        out_shape=(
            jax.ShapeDtypeStruct((TOK, D), BF16),
            jax.ShapeDtypeStruct((2, TOK), BF16),
            jax.ShapeDtypeStruct((HALF, LOCAL, 2 * FF), F32),
            jax.ShapeDtypeStruct((HALF, LOCAL, D), F32),
        ),
        in_specs=[hbm, vmem, hbm, hbm],
        out_specs=(hbm, vmem, hbm, hbm),
        scratch_shapes=[
            pltpu.VMEM((TOK, D), BF16),
            pltpu.VMEM((LOCAL, HALF, WIDE), BF16),
            pltpu.VMEM((LOCAL, 2, HALF, WIDE), BF16),
            pltpu.VMEM((HALF, LOCAL, 2 * FF), F32),
            pltpu.VMEM((HALF, LOCAL, D), F32),
            pltpu.SemaphoreType.DMA((2,)),
            pltpu.SemaphoreType.DMA((2, PARTS)),
            pltpu.SemaphoreType.DMA((2, PARTS)),
        ],
        compiler_params=pltpu.CompilerParams(vmem_limit_bytes=62 * 2**20),
        name="finish_sums",
    )(token_grad, combine_grad, own, arrived)
    return token_grad, combine_grad.T, inner, down


def solution(mesh):
    placed = (
        P(("dp", "expert"), None),
        P(("dp", "expert"), None),
        P(("dp", "expert"), None),
        P(("dp", "expert"), None),
        P(),
        P(None, "expert", None),
        P(None, "expert", None),
    )
    return jax.shard_map(
        on_device,
        mesh=mesh,
        in_specs=placed,
        out_specs=(
            P(("dp", "expert"), None),
            P(("dp", "expert"), None),
            P("dp", "expert", None),
            P("dp", "expert", None),
        ),
        check_vma=False,
    )
```

```python
import jax
import jax.numpy as jnp
from jax import lax
from jax.experimental import pallas as pl
from jax.experimental.pallas import tpu as pltpu
from jax.sharding import PartitionSpec as P

MESH = pl.DeviceIdType.MESH
BF16 = jnp.bfloat16
F32 = jnp.float32

D = 1024
FF = 1024
TOK = 256
CAP = 32
EXPERTS = 32
LOCAL = 2
PEERS = 16
SLOTS = PEERS * CAP
WIDE = 2 * FF + FF
HALF = 128
TILE = 256
RET = D + 128
GROUPS = 3
GROUP = WIDE // GROUPS
LAG = 3
STAGE = 128
PARTS = 4

PARTNERS = (
    (0, 0), (1, 0), (3, 0), (0, 1), (0, 3), (1, 1), (3, 3), (2, 2),
    (1, 3), (3, 1), (2, 0), (0, 2), (1, 2), (3, 2), (2, 1), (2, 3),
)
STEPS = (2, 1, 3, 0)


def dot(a, b):
    return lax.dot_general(a, b, (((1,), (0,)), ((), ())), preferred_element_type=F32)


def dot_nt(a, b):
    return lax.dot_general(a, b, (((1,), (1,)), ((), ())), preferred_element_type=F32)


def dot_tn(a, b):
    return lax.dot_general(a, b, (((0,), (0,)), ((), ())), preferred_element_type=F32)


def kernel(
    tokens_in, cotangent_in, combine_in, ids_in, capacity_in, w_in, w_down,
    token_out, combine_out, own, arrived,
    tokens, cotangent, combine, ids, capacity,
    raw_in, raw_down, win, wdown, pick0, pick1, send, recv, hidden, dpre, turned,
    part, core_sum, relay, ret_send, ret_recv,
    in_sem, raw_sem, send_sem, recv_sem, ret_send_sem, ret_recv_sem,
    core_send_sem, core_recv_sem, z_send_sem, z_recv_sem, keep_sem,
):
    dp = lax.axis_index("dp")
    ex = lax.axis_index("expert")
    z, core = dp // 2, dp % 2
    y, x = ex // 4, ex % 4

    def partner(i, sign):
        dx, dy = PARTNERS[i]
        return ((y + 4 + sign * dy) % 4) * 4 + (x + 4 + sign * dx) % 4

    def along_z(step):
        return (((z + step) % 4) * 2 + core, ex)

    sibling = (z * 2 + 1 - core, ex)

    def dispatch(e, i):
        return pltpu.make_async_remote_copy(
            src_ref=send.at[e, i], dst_ref=recv.at[e, i],
            send_sem=send_sem.at[e, i], recv_sem=recv_sem.at[e, i],
            device_id=(dp, partner(i, 1)), device_id_type=MESH,
        )

    def give_back(e, i):
        return pltpu.make_async_remote_copy(
            src_ref=ret_send.at[e, i], dst_ref=ret_recv.at[e, i],
            send_sem=ret_send_sem.at[e, i], recv_sem=ret_recv_sem.at[e, i],
            device_id=(dp, partner(i, -1)), device_id_type=MESH,
        )

    def group_cols(q):
        return pl.ds(q * GROUP, GROUP)

    def to_sibling(e, s, q):
        cols = group_cols(q)
        return pltpu.make_async_remote_copy(
            src_ref=part.at[s, 1 - core, :, cols], dst_ref=core_sum.at[e, s, :, cols],
            send_sem=core_send_sem.at[e, s, q], recv_sem=core_recv_sem.at[e, s, q],
            device_id=sibling, device_id_type=MESH,
        )

    half = HALF // 2

    def z_copy(e, k, q):
        cols, low, high = group_cols(q), pl.ds(0, half), pl.ds(half, half)
        src, dst, step = (
            (core_sum.at[e, 0, low, cols], relay.at[e, 0, :, cols], 1),
            (core_sum.at[e, 0, high, cols], relay.at[e, 1, :, cols], 3),
            (core_sum.at[e, 1, high, cols], arrived.at[e, 0, high, cols], 1),
            (core_sum.at[e, 2, low, cols], arrived.at[e, 1, low, cols], 3),
            (core_sum.at[e, 1, low, cols], arrived.at[e, 0, low, cols], 1),
            (core_sum.at[e, 2, high, cols], arrived.at[e, 1, high, cols], 3),
        )[k]
        return pltpu.make_async_remote_copy(
            src_ref=src, dst_ref=dst,
            send_sem=z_send_sem.at[e, k, q], recv_sem=z_recv_sem.at[e, k, q],
            device_id=along_z(step), device_id_type=MESH,
        )

    def keep(e):
        return pltpu.make_async_copy(core_sum.at[e, 3], own.at[e], keep_sem.at[e])

    def raw_copy(j, slot, which):
        src, dst = ((w_in, raw_in), (w_down, raw_down))[which]
        return pltpu.make_async_copy(
            src.at[pl.ds(pl.multiple_of(j * STAGE, STAGE), STAGE)], dst.at[slot],
            raw_sem.at[which, slot],
        )

    barrier = pltpu.get_barrier_semaphore()
    greeted = [(dp, partner(i, 1)) for i in range(1, PEERS)] + [sibling, along_z(1), along_z(3)]
    for device in greeted:
        pl.semaphore_signal(barrier, inc=1, device_id=device, device_id_type=MESH)

    fetched = [
        pltpu.make_async_copy(src, dst, in_sem.at[n])
        for n, (src, dst) in enumerate((
            (ids_in, ids), (capacity_in, capacity), (combine_in, combine),
            (tokens_in, tokens), (cotangent_in, cotangent),
        ))
    ]
    for copy in fetched:
        copy.start()
    for which in (0, 1):
        raw_copy(0, 0, which).start()
    for copy in fetched[:3]:
        copy.wait()

    rows = lax.broadcasted_iota(jnp.int32, (TOK, TOK), 0)
    columns = lax.broadcasted_iota(jnp.int32, (TOK, TOK), 1)
    earlier = (columns < rows).astype(F32).astype(BF16)
    lane = lax.broadcasted_iota(jnp.int32, (TOK, EXPERTS), 1)
    stood = jnp.concatenate(
        [ids[...].astype(F32), combine[...].astype(BF16).astype(F32), jnp.zeros((4, TOK), F32)], axis=0
    ).T
    id0, id1 = stood[:, 0:1].astype(jnp.int32), stood[:, 1:2].astype(jnp.int32)
    cb0, cb1 = stood[:, 2:3], stood[:, 3:4]
    named0 = (id0 == lane).astype(F32)
    named1 = (id1 == lane).astype(F32)
    before = dot(earlier, (named0 + named1).astype(BF16))
    limits = capacity[...].astype(F32)

    def target(named, number):
        position = jnp.sum(named * before, axis=1, keepdims=True)
        limit = jnp.sum(named * limits, axis=1, keepdims=True)
        return jnp.where(position < limit, number * CAP + position.astype(jnp.int32), -1)

    target0, target1 = target(named0, id0), target(named1, id1)
    slot_lane = lax.broadcasted_iota(jnp.int32, (1, SLOTS), 1)
    first = jnp.zeros((1, SLOTS), jnp.int32)
    for i in range(PEERS):
        first = jnp.where(slot_lane // CAP == i, partner(i, 1) * (LOCAL * CAP), first)
    first = first + slot_lane % CAP

    def choose(e):
        wanted = first + e * CAP
        pick0[e] = (target0 == wanted).astype(F32).astype(BF16)
        pick1[e] = (target1 == wanted).astype(F32).astype(BF16)

    choose(0)

    def gather(e, group):
        lanes = pl.ds(group * 128, 128)
        p0, p1 = pick0[e, :, lanes], pick1[e, :, lanes]
        for c in range(0, D, TILE):
            cols = pl.ds(c, TILE)
            cot = cotangent[:, cols].astype(F32)
            rows_x = dot_tn(p0 + p1, tokens[:, cols]).astype(BF16)
            rows_s = (
                dot_tn(p0, (cb0 * cot).astype(BF16)) + dot_tn(p1, (cb1 * cot).astype(BF16))
            ).astype(BF16)
            for j in range(4):
                i = group * 4 + j
                buffer = recv if i == 0 else send
                buffer[e, i, 0:CAP, cols] = rows_x[j * CAP:(j + 1) * CAP]
                buffer[e, i, CAP:2 * CAP, cols] = rows_s[j * CAP:(j + 1) * CAP]

    def start_dispatch(e, lo, hi):
        for i in range(max(lo, 1), hi):
            dispatch(e, i).start()

    for copy in fetched[3:]:
        copy.wait()
    for group in range(4):
        gather(0, group)
        if group == 0:
            pl.semaphore_wait(barrier, len(greeted))
        start_dispatch(0, group * 4, group * 4 + 4)
    choose(1)
    for group in range(4):
        gather(1, group)

    def settle(j, _):
        slot = j % 2

        @pl.when(j + 1 < D // STAGE)
        def _():
            for which in (0, 1):
                raw_copy(j + 1, 1 - slot, which).start()

        for which in (0, 1):
            raw_copy(j, slot, which).wait()

        def block(b, _):
            src = pl.multiple_of(b * 16, 16)
            dst = pl.ds(pl.multiple_of(j * STAGE + b * 16, 16), 16)
            win[:, dst, :] = jnp.swapaxes(raw_in[slot, pl.ds(src, 16)], 0, 1)
            wdown[:, dst, :] = jnp.swapaxes(raw_down[slot, pl.ds(src, 16)], 0, 1)
            return 0

        lax.fori_loop(0, STAGE // 16, block, 0)
        return 0

    lax.fori_loop(0, D // STAGE, settle, 0)

    def arrive(e, lo, hi):
        for i in range(max(lo, 1), hi):
            dispatch(e, i).wait_recv()

    def rows_of(e, h, lo, cols):
        return recv[e, h * 8:h * 8 + 8, lo:lo + CAP, cols].reshape(8 * CAP, -1)

    def forward(e, h):
        here = pl.ds(h * 256, 256)

        def tile(n, total):
            at = pl.multiple_of(n * TILE, TILE)
            cols, upper = pl.ds(at, TILE), pl.ds(FF + at, TILE)
            xs = rows_of(e, h, 0, slice(None))
            gate = dot(xs, win[e, :, cols])
            up = dot(xs, win[e, :, upper])
            dh = dot_nt(rows_of(e, h, CAP, slice(None)), wdown[e, cols, :])
            sig = jax.nn.sigmoid(gate)
            act = gate * sig
            hid = (act * up).astype(BF16)
            hidden[here, cols] = hid
            dpre[here, cols] = (dh * up * sig * (1.0 + gate * (1.0 - sig))).astype(BF16)
            dpre[here, upper] = (dh * act).astype(BF16)
            return total + jnp.sum(hid.astype(F32) * dh, axis=1, keepdims=True)

        total = lax.fori_loop(0, FF // TILE, tile, jnp.zeros((256, 1), F32), unroll=True)
        total = jnp.broadcast_to(total.astype(BF16), (256, 128)).reshape(8, CAP, 128)
        for j in range(8):
            i = h * 8 + j
            buffer = ret_recv if i == 0 else ret_send
            buffer[e, i, :, D:RET] = total[j]

    def partial(e, s, q):
        at = pl.multiple_of(((z + STEPS[s]) % 4) * TILE, TILE)
        if q == 0:
            turned[...] = recv[e, :, 0:CAP, pl.ds(at, TILE)].reshape(SLOTS, TILE).T
        if q == 2:
            turned[...] = hidden[:, pl.ds(at, TILE)].T

        def tile(n, _):
            at = pl.multiple_of(n * TILE, TILE)
            if q < 2:
                other = dpre[:, pl.ds(q * GROUP + at, TILE)]
            else:
                other = recv[e, :, CAP:2 * CAP, pl.ds(at, TILE)].reshape(SLOTS, TILE)
            part[s, :, :, pl.ds(q * GROUP + at, TILE)] = (
                dot(turned[...], other).astype(BF16).reshape(2, HALF, TILE)
            )
            return 0

        lax.fori_loop(0, GROUP // TILE, tile, 0, unroll=True)

    def add_rows(dst, lo, count, other, q):
        cols = group_cols(q)

        def block(b, _):
            at = pl.multiple_of(b * 16, 16)
            here = dst[pl.ds(lo + at, 16), cols].astype(F32)
            there = other[pl.ds(at, 16), cols].astype(F32)
            dst[pl.ds(lo + at, 16), cols] = (here + there).astype(BF16)
            return 0

        lax.fori_loop(0, count // 16, block, 0)

    def meet_sibling(e, s, q):
        to_sibling(e, s, q).wait_recv()
        add_rows(core_sum.at[e, s], 0, HALF, part.at[s, core], q)
        for k in ((0, 1), (2,), (3,), ())[s]:
            z_copy(e, k, q).start()

    def weight_sums(e):
        units = [(s, q) for s in range(4) for q in range(GROUPS)]
        for n, unit in enumerate(units):
            partial(e, *unit)
            to_sibling(e, *unit).start()
            if n >= LAG:
                meet_sibling(e, *units[n - LAG])
        for unit in units[-LAG:]:
            meet_sibling(e, *unit)
        keep(e).start()

    def pass_on(e, q):
        z_copy(e, 0, q).wait_recv()
        add_rows(core_sum.at[e, 1], 0, half, relay.at[e, 0], q)
        z_copy(e, 4, q).start()
        z_copy(e, 1, q).wait_recv()
        add_rows(core_sum.at[e, 2], half, half, relay.at[e, 1], q)
        z_copy(e, 5, q).start()

    def input_grad(e, h):
        def tile(n, _):
            cols = pl.ds(pl.multiple_of(n * TILE, TILE), TILE)
            grad = dot_nt(dpre[pl.ds(h * 256, 256), :], win[e, cols, :]).astype(BF16)
            grad = grad.reshape(8, CAP, TILE)
            for j in range(8):
                i = h * 8 + j
                buffer = ret_recv if i == 0 else ret_send
                buffer[e, i, :, cols] = grad[j]
            return 0

        lax.fori_loop(0, D // TILE, tile, 0, unroll=True)
        for i in range(max(h * 8, 1), h * 8 + 8):
            give_back(e, i).start()

    arrive(0, 0, 8)
    start_dispatch(1, 0, PEERS)
    forward(0, 0)
    arrive(0, 8, PEERS)
    forward(0, 1)
    weight_sums(0)
    input_grad(0, 0)
    input_grad(0, 1)
    pass_on(0, 0)
    arrive(1, 0, 8)
    forward(1, 0)
    pass_on(0, 1)
    pass_on(0, 2)
    arrive(1, 8, PEERS)
    forward(1, 1)
    for s in range(4):
        for q in range(GROUPS):
            to_sibling(0, s, q).wait_send()
    weight_sums(1)
    input_grad(1, 0)
    pass_on(1, 0)
    input_grad(1, 1)
    pass_on(1, 1)
    pass_on(1, 2)

    for e in range(LOCAL):
        for i in range(1, PEERS):
            give_back(e, i).wait_recv()
    for c in range(0, D, TILE):
        cols = pl.ds(c, TILE)
        total = jnp.zeros((TOK, TILE), F32)
        for e in range(LOCAL):
            total = total + dot(
                pick0[e] + pick1[e], ret_recv[e, :, :, cols].reshape(SLOTS, TILE)
            )
        token_out[:, cols] = total.astype(BF16)
    router = []
    for pick, cb in ((pick0, cb0), (pick1, cb1)):
        total = jnp.zeros((TOK, 128), F32)
        for e in range(LOCAL):
            total = total + dot(pick[e], ret_recv[e, :, :, D:RET].reshape(SLOTS, 128))
        router.append(total[:, 0:1] / cb)
    router = jnp.concatenate(router + [jnp.zeros((TOK, 6), F32)], axis=1)
    combine_out[...] = router.T[0:2].astype(BF16)

    for e in range(LOCAL):
        for i in range(1, PEERS):
            dispatch(e, i).wait_send()
            give_back(e, i).wait_send()
        for q in range(GROUPS):
            for k in range(6):
                z_copy(e, k, q).wait_send()
            for k in (2, 3, 4, 5):
                z_copy(e, k, q).wait_recv()
        keep(e).wait()
    for s in range(4):
        for q in range(GROUPS):
            to_sibling(1, s, q).wait_send()


def finish(
    token_in, combine_in, own_in, arrived_in, token_out, combine_out, inner_out, down_out,
    token, own, arrived, inner, down, token_sem, in_sem, out_sem,
):
    rows = HALF // PARTS
    fetched = pltpu.make_async_copy(token_in, token, token_sem.at[0])
    passed = pltpu.make_async_copy(token, token_out, token_sem.at[1])
    fetched.start()

    def load(p):
        here = pl.ds(p * rows, rows)
        return (
            pltpu.make_async_copy(own_in.at[:, here], own.at[:, here], in_sem.at[0, p]),
            pltpu.make_async_copy(arrived_in.at[:, :, here], arrived.at[:, :, here], in_sem.at[1, p]),
        )

    def store(p):
        here = pl.ds(p * rows, rows)
        return (
            pltpu.make_async_copy(inner.at[here], inner_out.at[here], out_sem.at[0, p]),
            pltpu.make_async_copy(down.at[here], down_out.at[here], out_sem.at[1, p]),
        )

    for p in range(PARTS):
        for copy in load(p):
            copy.start()
    combine_out[...] = combine_in[...]
    fetched.wait()
    passed.start()
    for p in range(PARTS):
        for copy in load(p):
            copy.wait()

        def block(b, _):
            at = pl.ds(pl.multiple_of(p * rows + b * 16, 16), 16)
            total = own[:, at].astype(F32)
            total = total + arrived[:, 0, at].astype(F32) + arrived[:, 1, at].astype(F32)
            total = jnp.swapaxes(total, 0, 1)
            inner[at] = total[..., :2 * FF]
            down[at] = total[..., 2 * FF:]
            return 0

        lax.fori_loop(0, rows // 16, block, 0)
        for copy in store(p):
            copy.start()
    passed.wait()
    for p in range(PARTS):
        for copy in store(p):
            copy.wait()


def on_device(tokens, cotangent, combine, expert_ids, capacity, weight_in, weight_down):
    vmem = pl.BlockSpec(memory_space=pltpu.VMEM)
    hbm = pl.BlockSpec(memory_space=pl.ANY)
    token_grad, combine_grad, own, arrived = pl.pallas_call(
        kernel,
        out_shape=(
            jax.ShapeDtypeStruct((TOK, D), BF16),
            jax.ShapeDtypeStruct((2, TOK), BF16),
            jax.ShapeDtypeStruct((LOCAL, HALF, WIDE), BF16),
            jax.ShapeDtypeStruct((LOCAL, 2, HALF, WIDE), BF16),
        ),
        in_specs=[hbm] * 7,
        out_specs=(vmem, vmem, hbm, hbm),
        scratch_shapes=[
            pltpu.VMEM((TOK, D), BF16),
            pltpu.VMEM((TOK, D), BF16),
            pltpu.VMEM((2, TOK), F32),
            pltpu.VMEM((2, TOK), jnp.int32),
            pltpu.VMEM((1, EXPERTS), jnp.int32),
            pltpu.VMEM((2, STAGE, LOCAL, 2 * FF), BF16),
            pltpu.VMEM((2, STAGE, LOCAL, D), BF16),
            pltpu.VMEM((LOCAL, D, 2 * FF), BF16),
            pltpu.VMEM((LOCAL, FF, D), BF16),
            pltpu.VMEM((LOCAL, TOK, SLOTS), BF16),
            pltpu.VMEM((LOCAL, TOK, SLOTS), BF16),
            pltpu.VMEM((LOCAL, PEERS, 2 * CAP, D), BF16),
            pltpu.VMEM((LOCAL, PEERS, 2 * CAP, D), BF16),
            pltpu.VMEM((SLOTS, FF), BF16),
            pltpu.VMEM((SLOTS, 2 * FF), BF16),
            pltpu.VMEM((TILE, SLOTS), BF16),
            pltpu.VMEM((4, 2, HALF, WIDE), BF16),
            pltpu.VMEM((LOCAL, 4, HALF, WIDE), BF16),
            pltpu.VMEM((LOCAL, 2, HALF // 2, WIDE), BF16),
            pltpu.VMEM((LOCAL, PEERS, CAP, RET), BF16),
            pltpu.VMEM((LOCAL, PEERS, CAP, RET), BF16),
            pltpu.SemaphoreType.DMA((5,)),
            pltpu.SemaphoreType.DMA((2, 2)),
            pltpu.SemaphoreType.DMA((LOCAL, PEERS)),
            pltpu.SemaphoreType.DMA((LOCAL, PEERS)),
            pltpu.SemaphoreType.DMA((LOCAL, PEERS)),
            pltpu.SemaphoreType.DMA((LOCAL, PEERS)),
            pltpu.SemaphoreType.DMA((LOCAL, 4, GROUPS)),
            pltpu.SemaphoreType.DMA((LOCAL, 4, GROUPS)),
            pltpu.SemaphoreType.DMA((LOCAL, 6, GROUPS)),
            pltpu.SemaphoreType.DMA((LOCAL, 6, GROUPS)),
            pltpu.SemaphoreType.DMA((LOCAL,)),
        ],
        compiler_params=pltpu.CompilerParams(
            collective_id=0, has_side_effects=True, vmem_limit_bytes=62 * 2**20
        ),
        name="moe_backward",
    )(
        tokens, cotangent, combine.T, expert_ids.T, capacity.reshape(1, EXPERTS),
        weight_in, weight_down,
    )
    token_grad, combine_grad, inner, down = pl.pallas_call(
        finish,
        out_shape=(
            jax.ShapeDtypeStruct((TOK, D), BF16),
            jax.ShapeDtypeStruct((2, TOK), BF16),
            jax.ShapeDtypeStruct((HALF, LOCAL, 2 * FF), F32),
            jax.ShapeDtypeStruct((HALF, LOCAL, D), F32),
        ),
        in_specs=[hbm, vmem, hbm, hbm],
        out_specs=(hbm, vmem, hbm, hbm),
        scratch_shapes=[
            pltpu.VMEM((TOK, D), BF16),
            pltpu.VMEM((LOCAL, HALF, WIDE), BF16),
            pltpu.VMEM((LOCAL, 2, HALF, WIDE), BF16),
            pltpu.VMEM((HALF, LOCAL, 2 * FF), F32),
            pltpu.VMEM((HALF, LOCAL, D), F32),
            pltpu.SemaphoreType.DMA((2,)),
            pltpu.SemaphoreType.DMA((2, PARTS)),
            pltpu.SemaphoreType.DMA((2, PARTS)),
        ],
        compiler_params=pltpu.CompilerParams(vmem_limit_bytes=62 * 2**20),
        name="finish_sums",
    )(token_grad, combine_grad, own, arrived)
    return token_grad, combine_grad.T, inner, down


def solution(mesh):
    placed = (
        P(("dp", "expert"), None),
        P(("dp", "expert"), None),
        P(("dp", "expert"), None),
        P(("dp", "expert"), None),
        P(),
        P(None, "expert", None),
        P(None, "expert", None),
    )
    return jax.shard_map(
        on_device,
        mesh=mesh,
        in_specs=placed,
        out_specs=(
            P(("dp", "expert"), None),
            P(("dp", "expert"), None),
            P("dp", "expert", None),
            P("dp", "expert", None),
        ),
        check_vma=False,
    )
```
